512 devices in a mesh: kx: 8 (over x, z_lo), ky: 8 (over z_hi, core), kz: 8 (over y).
Axes of the slice: x: 4, y: 8, z: 8 (z_hi: 4, z_lo: 2; z = z_hi * 2 + z_lo), core: 2. Of those that a mesh axis runs over, the one named last changes fastest.
Arguments:
- coeffs: bfloat16 [8, 8, 8, 128, 2, 4096], P('kx', 'ky', 'kz'), may hold values from -0.62890625 to 0.62890625
- slab_maps: int32 [8, 8, 8, 3, 32], P('kx', 'ky', 'kz'), may hold values from 0 to 31, each once within a row
Outputs:
- correlations: float32 [8, 8, 8, 6, 2, 128, 128], P('kx', 'ky', 'kz')
The draws below stay inside these ranges and needn't reach their ends.
Inputs may be any that keep to these rules, and one draw needn't show every extreme that they name: Each row slab_maps[kx, ky, kz, d, :] holds every number of 0 to 31 once.
All inputs are finite; a program needn't handle non-finite values.
Results may differ from the reference program's by a relative error of at most 0.0003.
Values may be sent and summed in bfloat16 or wider, within the bound.
No kernel may reach another device: no remote copies, remote signals or barrier semaphores. Data moves between devices by JAX's collectives and lax.ppermute only.
A program may use at most 64 MiB of HBM per device.

```python
import jax
import jax.numpy as jnp
from jax import lax

BANDS = 128
PW = 4096
NSLAB = 32
NKX = 8
NKY = 8
NKZ = 8


def steps_of(own_key, dims, split, smallest, largest):
    gain = 1.0
    for axis_at, shards_of in split:
        heights = jax.random.uniform(jax.random.fold_in(jax.random.fold_in(own_key, 6), axis_at), (shards_of,), jnp.float32, smallest / len(split), largest / len(split))
        gain = gain * jnp.repeat(jnp.exp(heights), dims[axis_at] // shards_of).reshape((-1,) + (1,) * (len(dims) - 1 - axis_at))
    return gain


def normal_values(rng, dims, scale, limit, cuts=(), kind=jnp.bfloat16):
    level = steps_of(rng, dims, cuts, -0.22, 0.18) if cuts else 1.0
    values = jax.random.normal(rng, dims, jnp.float32) * scale * level
    return jnp.minimum(jnp.maximum(values, -limit), limit).astype(kind)


def setup_inputs(seed: int = 0) -> dict:
    splits = jax.random.split(jax.random.key(seed), 3)
    coeffs = normal_values(splits[0], (NKX, NKY, NKZ, BANDS, 2, PW), ((2 * PW) ** -0.25), 0.62890625, ((0, 8), (1, 8), (2, 8)))
    slab_maps = jax.vmap(lambda own: jax.random.permutation(own, NSLAB))(jax.random.split(splits[1], NKX * NKY * NKZ * 3)).reshape((NKX, NKY, NKZ, 3, NSLAB)).astype(jnp.int32)
    return dict(coeffs=coeffs, slab_maps=slab_maps)


def permute(values, order):
    bands, parts, width = values.shape
    count = order.shape[0]
    blocks = values.reshape(bands, parts, count, width // count)
    return jnp.take(blocks, order, axis=2).reshape(bands, parts, width)


def product(left, right):
    return lax.dot_general(left, right, (((1,), (1,)), ((), ())), preferred_element_type=jnp.float32)


def correlation(left, right):
    real = product(left[:, 0], right[:, 0]) + product(left[:, 1], right[:, 1])
    imag = product(left[:, 0], right[:, 1]) - product(left[:, 1], right[:, 0])
    return jnp.stack([real, imag])


def reference(coeffs, slab_maps):
    nx, ny, nz = coeffs.shape[0], coeffs.shape[1], coeffs.shape[2]

    def single(index):
        ix = index // (ny * nz)
        iy = (index // nz) % ny
        iz = index % nz
        here = coeffs[ix, iy, iz]
        forward = []
        backward = []
        for direction, step in enumerate(((1, 0, 0), (0, 1, 0), (0, 0, 1))):
            ahead = coeffs[(ix + step[0]) % nx, (iy + step[1]) % ny, (iz + step[2]) % nz]
            forward.append(correlation(here, permute(ahead, slab_maps[ix, iy, iz, direction])))
            bx = (ix - step[0]) % nx
            by = (iy - step[1]) % ny
            bz = (iz - step[2]) % nz
            behind = coeffs[bx, by, bz]
            backward.append(correlation(permute(here, slab_maps[bx, by, bz, direction]), behind))
        return jnp.stack(forward + backward)

    result = lax.map(single, jnp.arange(nx * ny * nz, dtype=jnp.int32))
    return result.reshape(nx, ny, nz, 6, 2, BANDS, BANDS)
```

```python
import jax
import jax.numpy as jnp
from jax import lax
from jax.experimental import pallas as pl
from jax.experimental.pallas import tpu as pltpu
from jax.sharding import PartitionSpec as P

AXES = ("kx", "ky", "kz")
BANDS, PARTS, WIDTH, SLABS, LANES = 128, 2, 4096, 32, 128
ROWS = BANDS * PARTS
BLOCKS = 4
PER = SLABS // BLOCKS
TAIL = 16
BLOCK_ROWS = PER * ROWS + TAIL
F32 = jnp.float32
NT = (((1,), (1,)), ((), ()))
VMEM = pl.BlockSpec(memory_space=pltpu.VMEM)
SMEM = pl.BlockSpec(memory_space=pltpu.SMEM)


def routes(nx, ny, nz):
    def at(a, b, c):
        return ((a % nx) * ny + b % ny) * nz + c % nz

    square, cross, along, column = [], [], [], []
    for a in range(nx):
        for b in range(ny):
            for c in range(nz):
                me, high, core = at(a, b, c), a % 2, b % 2
                if high == core:
                    square.append((me, at(a, b - 1, c) if high else at(a, b + 1, c)))
                    cross.append((me, at(a - 1, b + 1, c) if high else at(a + 1, b - 1, c)))
                    along.append((me, at(a + 2, b, c) if high else at(a - 2, b, c)))
                else:
                    square.append((me, at(a - 1, b, c) if high else at(a + 1, b, c)))
                column.append((me, at(a, b, c - 1) if core else at(a, b, c + 1)))
    return square, cross, along, column


def back(route):
    return [(t, s) for s, t in route]


def send(x, route):
    return lax.ppermute(x, AXES, route)


def pack_kernel(u_ref, maps_ref, out_ref):
    for s in range(PER):
        out_ref[s * ROWS : (s + 1) * ROWS] = u_ref[:, :, s * LANES : (s + 1) * LANES].reshape(ROWS, LANES)
    out_ref[PER * ROWS :] = maps_ref[...].astype(F32).astype(jnp.bfloat16)


def packed(u, maps):
    padded = jnp.pad(maps, ((0, TAIL - maps.shape[0]), (0, LANES - SLABS)))
    return pl.pallas_call(
        pack_kernel,
        grid=(BLOCKS,),
        in_specs=[
            pl.BlockSpec((BANDS, PARTS, WIDTH // BLOCKS), lambda i: (0, 0, i)),
            pl.BlockSpec((TAIL, LANES), lambda i: (0, 0)),
        ],
        out_specs=pl.BlockSpec((BLOCK_ROWS, LANES), lambda i: (i, 0)),
        out_shape=jax.ShapeDtypeStruct((BLOCKS * BLOCK_ROWS, LANES), jnp.bfloat16),
        compiler_params=pltpu.CompilerParams(vmem_limit_bytes=16 << 20),
        cost_estimate=pl.CostEstimate(flops=0, bytes_accessed=4 << 20, transcendentals=0),
    )(u, padded)


def slab(ref, index):
    row = index * ROWS + lax.div(index, PER) * TAIL
    return ref[pl.ds(pl.multiple_of(row, 16), ROWS), :]


def edge_kernel(flags_ref, p_ref, q_ref, t_ref, h_ref, ints, order, g_ref, s_ref, sem):
    first = flags_ref[0]

    @pl.when(flags_ref[1] == 1)
    def _():
        tail = pl.ds(PER * ROWS, TAIL)
        chosen = jnp.where(first == 1, p_ref[tail, :].astype(F32), q_ref[tail, :].astype(F32))
        ints[...] = chosen.astype(jnp.int32)
        copy = pltpu.make_async_copy(ints, order, sem)
        copy.start()
        copy.wait()
        left, right = [], []
        for s in range(SLABS):
            other = order[flags_ref[2], s]
            left.append(slab(p_ref, jnp.where(first == 1, s, other)))
            right.append(slab(q_ref, jnp.where(first == 1, other, s)))
        g = lax.dot_general(
            jnp.concatenate(left, axis=1), jnp.concatenate(right, axis=1), NT, preferred_element_type=F32
        )
        for half in range(2):
            g_ref[half] = g[:, half * LANES : (half + 1) * LANES]
        for half in range(2):
            for part in range(2):
                s_ref[part, half * LANES : (half + 1) * LANES] = g_ref[half, pl.ds(part, BANDS, stride=2), :].T
        rr, ri = s_ref[0, pl.ds(0, BANDS, stride=2), :], s_ref[0, pl.ds(1, BANDS, stride=2), :]
        ir, ii = s_ref[1, pl.ds(0, BANDS, stride=2), :], s_ref[1, pl.ds(1, BANDS, stride=2), :]
        real, imag = rr + ii, ri - ir
        h_ref[0] = real
        h_ref[1] = -imag
        t_ref[0] = real.T
        t_ref[1] = imag.T


def edge(direction, first, runs, p, q):
    flags = jnp.stack([first, runs, direction]).astype(jnp.int32)
    shape = jax.ShapeDtypeStruct((PARTS, BANDS, BANDS), F32)
    return pl.pallas_call(
        edge_kernel,
        in_specs=[SMEM, VMEM, VMEM],
        out_specs=[VMEM, VMEM],
        out_shape=[shape, shape],
        scratch_shapes=[
            pltpu.VMEM((TAIL, LANES), jnp.int32),
            pltpu.SMEM((TAIL, LANES), jnp.int32),
            pltpu.VMEM((2, ROWS, LANES), F32),
            pltpu.VMEM((2, ROWS, LANES), F32),
            pltpu.SemaphoreType.DMA,
        ],
        compiler_params=pltpu.CompilerParams(vmem_limit_bytes=16 << 20),
        cost_estimate=pl.CostEstimate(
            flops=2 * ROWS * ROWS * WIDTH, bytes_accessed=4 << 20, transcendentals=0
        ),
    )(flags, p, q)


def gather_kernel(role_ref, k1, k4, r1, r2, r3, r4, out_ref, sems):
    three = [r1.at[i] for i in range(3)]
    places = {
        0: [k1, three[0], r4, r3, r2, k4],
        1: [three[0], three[1], k4, three[2], k1, r4],
        2: [three[2], k1, r4, three[0], three[1], k4],
        3: [r3, r2, k4, k1, three[0], r4],
    }
    for role, sources in places.items():

        @pl.when(role_ref[0] == role)
        def _():
            copies = [pltpu.make_async_copy(x, out_ref.at[i], sems.at[i]) for i, x in enumerate(sources)]
            for c in copies:
                c.start()
            for c in copies:
                c.wait()


def gathered(role, *parts):
    any_ = pl.BlockSpec(memory_space=pl.ANY)
    return pl.pallas_call(
        gather_kernel,
        in_specs=[SMEM] + [any_] * len(parts),
        out_specs=any_,
        out_shape=jax.ShapeDtypeStruct((6, PARTS, BANDS, BANDS), F32),
        scratch_shapes=[pltpu.SemaphoreType.DMA((6,))],
        compiler_params=pltpu.CompilerParams(vmem_limit_bytes=4 << 20),
        cost_estimate=pl.CostEstimate(flops=0, bytes_accessed=2 << 20, transcendentals=0),
    )(role[None], *parts)


def per_device(coeffs, slab_maps):
    square, cross, along, column = routes(*(lax.axis_size(a) for a in AXES))
    high = lax.axis_index("kx") % 2
    core = lax.axis_index("ky") % 2
    hub = (high == core).astype(jnp.int32)
    one = jnp.ones_like(hub)
    own = packed(coeffs[0, 0, 0], slab_maps[0, 0, 0])
    from_square = send(own, square)
    from_cross = send(own, cross)
    from_along = send(own, along)
    from_column = send(own, column)
    t1, h1 = edge(1 - hub, 1 - core, one, own, from_square)
    t2, h2 = edge(1, high, hub, from_square, from_cross)
    t3, h3 = edge(0, 1 - high, hub, from_square, from_along)
    t4, h4 = edge(2, core, one, own, from_column)
    back_square = send(jnp.stack([h1, t2, t3]), back(square))
    back_cross = send(h2, back(cross))
    back_along = send(h3, back(along))
    back_column = send(h4, back(column))
    out = gathered(2 * high + core, t1, t4, back_square, back_cross, back_along, back_column)
    return out[None, None, None]


def solution(mesh):
    placed = (P("kx", "ky", "kz", None, None, None), P("kx", "ky", "kz", None, None))
    return jax.shard_map(
        per_device,
        mesh=mesh,
        in_specs=placed,
        out_specs=P("kx", "ky", "kz", None, None, None, None),
        check_vma=False,
    )
```

```python
import jax
import jax.numpy as jnp
from jax import lax
from jax.experimental import pallas as pl
from jax.experimental.pallas import tpu as pltpu
from jax.sharding import PartitionSpec as P

AXES = ("kx", "ky", "kz")
BANDS, PARTS, WIDTH, SLABS, LANES = 128, 2, 4096, 32, 128
ROWS = BANDS * PARTS
BLOCKS = 8
PER = SLABS // BLOCKS
TAIL = 16
F32 = jnp.float32
COST = 1024
NT = (((1,), (1,)), ((), ()))
ANY = pl.BlockSpec(memory_space=pl.ANY)
VMEM = pl.BlockSpec(memory_space=pltpu.VMEM)
HBM = pl.BlockSpec(memory_space=pltpu.HBM)
RESULT = jax.ShapeDtypeStruct((PARTS, BANDS, BANDS), F32)
QUAD = jax.ShapeDtypeStruct((4, PARTS, BANDS, BANDS), F32)
RESULTS = jax.ShapeDtypeStruct((3, PARTS, BANDS, BANDS), F32)


def routes(nx, ny, nz):
    def at(a, b, c):
        return ((a % nx) * ny + b % ny) * nz + c % nz

    square, cross, along, lift = [], [], [], []
    for a in range(nx):
        for b in range(ny):
            for c in range(nz):
                me, high, core = at(a, b, c), a % 2, b % 2
                up = c - 1 if core else c + 1
                if high == core:
                    square.append((me, at(a, b - 1, c) if high else at(a, b + 1, c)))
                    cross.append((me, at(a - 1, b + 1, c) if high else at(a + 1, b - 1, c)))
                    along.append((me, at(a + 2, b, c) if high else at(a - 2, b, c)))
                    lift.append((me, at(a, b - 1 if core else b + 1, up)))
                else:
                    square.append((me, at(a - 1, b, c) if high else at(a + 1, b, c)))
                    cross.append((me, at(a, b, up)))
    return square, cross, along, lift


def back(route):
    return [(t, s) for s, t in route]


def send(x, route):
    return lax.ppermute(x, AXES, route)


def place():
    return lax.rem(lax.axis_index("kx"), 2), lax.rem(lax.axis_index("ky"), 2)


def pack_kernel(u_ref, maps_ref, out_ref, raw, ready, maps, ints, in_sems, out_sems, sem):
    width = PER * LANES
    loads = [
        pltpu.make_async_copy(u_ref.at[:, :, pl.ds(i * width, width)], raw.at[i], in_sems.at[i])
        for i in range(BLOCKS)
    ]
    stores = [
        pltpu.make_async_copy(ready.at[i], out_ref.at[pl.ds(i * PER * ROWS, PER * ROWS), :], out_sems.at[i])
        for i in range(BLOCKS)
    ]
    table = pltpu.make_async_copy(maps_ref, maps, sem)
    table.start()
    for c in loads:
        c.start()
    ints[...] = jnp.zeros_like(ints)
    table.wait()
    for d in range(maps.shape[0]):
        ints[d : d + 1, :SLABS] = maps[d]
    ready[BLOCKS, :TAIL, :] = ints[...].astype(F32).astype(jnp.bfloat16)
    tail = pltpu.make_async_copy(ready.at[BLOCKS, pl.ds(0, TAIL), :], out_ref.at[pl.ds(SLABS * ROWS, TAIL), :], sem)
    tail.start()
    for i in range(BLOCKS):
        loads[i].wait()
        for s in range(PER):
            ready[i, s * ROWS : (s + 1) * ROWS, :] = raw[i, :, :, s * LANES : (s + 1) * LANES].reshape(ROWS, LANES)
        stores[i].start()
    tail.wait()
    for c in stores:
        c.wait()


def packed(u, maps):
    return pl.pallas_call(
        pack_kernel,
        in_specs=[ANY, ANY],
        out_specs=ANY,
        out_shape=jax.ShapeDtypeStruct((SLABS * ROWS + TAIL, LANES), jnp.bfloat16),
        scratch_shapes=[
            pltpu.VMEM((BLOCKS, BANDS, PARTS, PER * LANES), jnp.bfloat16),
            pltpu.VMEM((BLOCKS + 1, PER * ROWS, LANES), jnp.bfloat16),
            pltpu.VMEM((maps.shape[0], 1, SLABS), jnp.int32),
            pltpu.VMEM((TAIL, LANES), jnp.int32),
            pltpu.SemaphoreType.DMA((BLOCKS,)),
            pltpu.SemaphoreType.DMA((BLOCKS,)),
            pltpu.SemaphoreType.DMA,
        ],
        compiler_params=pltpu.CompilerParams(vmem_limit_bytes=61 << 20),
        cost_estimate=pl.CostEstimate(flops=0, bytes_accessed=4 << 20, transcendentals=0),
    )(u, maps[:, None, :])


def keep_kernel(own, out_ref, sem):
    copy = pltpu.make_async_copy(own, out_ref, sem)
    copy.start()
    copy.wait()


def kept(own):
    return pl.pallas_call(
        keep_kernel,
        in_specs=[ANY],
        out_specs=VMEM,
        out_shape=jax.ShapeDtypeStruct(own.shape, own.dtype),
        scratch_shapes=[pltpu.SemaphoreType.DMA],
        compiler_params=pltpu.CompilerParams(vmem_limit_bytes=16 << 20),
        cost_estimate=pl.CostEstimate(flops=0, bytes_accessed=4 << 20, transcendentals=0),
    )(own)


def slab(ref, index):
    return ref[pl.ds(pl.multiple_of(index * ROWS, ROWS), ROWS), :]


def multiply(p_ref, q_ref, first, direction, ints, order, g_ref, s_ref, sem):
    tail = pl.ds(SLABS * ROWS, TAIL)
    ints[...] = jnp.where(first, p_ref[tail, :].astype(F32), q_ref[tail, :].astype(F32)).astype(jnp.int32)
    copy = pltpu.make_async_copy(ints, order, sem)
    copy.start()
    copy.wait()
    left, right = [], []
    for s in range(SLABS):
        other = order[direction, s]
        left.append(slab(p_ref, jnp.where(first, s, other)))
        right.append(slab(q_ref, jnp.where(first, other, s)))
    g = lax.dot_general(
        jnp.concatenate(left, axis=1), jnp.concatenate(right, axis=1), NT, preferred_element_type=F32
    )
    for half in range(2):
        g_ref[half] = g[:, half * LANES : (half + 1) * LANES]
    for half in range(2):
        for part in range(2):
            s_ref[part, half * LANES : (half + 1) * LANES] = g_ref[half, pl.ds(part, BANDS, stride=2), :].T
    rr, ri = s_ref[0, pl.ds(0, BANDS, stride=2), :], s_ref[0, pl.ds(1, BANDS, stride=2), :]
    ir, ii = s_ref[1, pl.ds(0, BANDS, stride=2), :], s_ref[1, pl.ds(1, BANDS, stride=2), :]
    return rr + ii, ri - ir


def put(t_ref, h_ref, real, imag):
    h_ref[0] = real
    h_ref[1] = -imag
    t_ref[0] = real.T
    t_ref[1] = imag.T


def square_kernel(own, square, t_ref, b_ref, *scratch):
    high, core = place()
    put(t_ref, b_ref.at[0], *multiply(own, square, core == 0, jnp.where(high == core, 0, 1), *scratch))


def cross_kernel(own, square, cross, _, b_ref, h_ref, *scratch):
    high, core = place()

    @pl.when(high == core)
    def _():
        put(b_ref.at[2], h_ref, *multiply(square, cross, high == 1, 1, *scratch))

    @pl.when(high != core)
    def _():
        put(b_ref.at[2], h_ref, *multiply(own, cross, core == 1, 2, *scratch))


def along_kernel(square, along, lift, _, b_ref, h_ref, *scratch):
    high, core = place()

    @pl.when(high == core)
    def _():
        put(b_ref.at[1], h_ref.at[0], *multiply(square, along, high == 0, 0, *scratch))

    @pl.when(high != core)
    def _():
        put(b_ref.at[1], h_ref.at[0], *multiply(square, lift, core == 0, 2, *scratch))


def multiplier(kernel, outs, buffers, results=None):
    operands = list(buffers) if results is None else [*buffers, results]
    return pl.pallas_call(
        kernel,
        in_specs=[VMEM] * len(operands),
        out_specs=[VMEM] * len(outs),
        out_shape=outs,
        input_output_aliases={} if results is None else {len(buffers): 0},
        scratch_shapes=[
            pltpu.VMEM((TAIL, LANES), jnp.int32),
            pltpu.SMEM((TAIL, LANES), jnp.int32),
            pltpu.VMEM((2, ROWS, LANES), F32),
            pltpu.VMEM((2, ROWS, LANES), F32),
            pltpu.SemaphoreType.DMA,
        ],
        compiler_params=pltpu.CompilerParams(vmem_limit_bytes=16 << 20),
        cost_estimate=pl.CostEstimate(
            flops=COST, bytes_accessed=COST, transcendentals=0
        ),
    )(*operands)


def gather_kernel(t1, mine, r_square, r_cross, r_along, r_lift, out_ref, sems):
    high, core = place()
    three = [r_square.at[i] for i in range(3)]
    r_along, r_lift = r_along.at[0], r_lift.at[0]
    places = {
        0: [t1, three[0], r_lift, r_along, r_cross, three[1]],
        1: [three[0], three[2], mine.at[2], three[1], t1, r_cross],
        2: [three[1], t1, r_cross, three[0], three[2], mine.at[2]],
        3: [r_along, r_cross, three[1], t1, three[0], r_lift],
    }
    for role, sources in places.items():

        @pl.when(2 * high + core == role)
        def _():
            copies = [pltpu.make_async_copy(x, out_ref.at[i], sems.at[i]) for i, x in enumerate(sources)]
            for c in copies:
                c.start()
            for c in copies:
                c.wait()


def gathered(*parts):
    return pl.pallas_call(
        gather_kernel,
        in_specs=[ANY] * len(parts),
        out_specs=ANY,
        out_shape=jax.ShapeDtypeStruct((6, PARTS, BANDS, BANDS), F32),
        scratch_shapes=[pltpu.SemaphoreType.DMA((6,))],
        compiler_params=pltpu.CompilerParams(vmem_limit_bytes=4 << 20),
        cost_estimate=pl.CostEstimate(flops=0, bytes_accessed=COST, transcendentals=0),
    )(*parts)


def per_device(coeffs, slab_maps):
    square, cross, along, lift = routes(*(lax.axis_size(a) for a in AXES))
    own = packed(coeffs[0, 0, 0], slab_maps[0, 0, 0])
    from_square = send(own, square)
    from_cross = send(own, cross)
    from_along = send(own, along)
    from_lift = send(own, lift)
    own = kept(own)
    t1, results = multiplier(square_kernel, [RESULT, RESULTS], [own, from_square])
    results, h3 = multiplier(along_kernel, [RESULTS, QUAD], [from_square, from_along, from_lift], results)
    results, h2 = multiplier(cross_kernel, [RESULTS, RESULT], [own, from_square, from_cross], results)
    back_cross = send(h2, back(cross))
    back_square = send(results, back(square))
    back_along = send(h3, back(along))
    back_lift = send(h3, back(lift))
    out = gathered(t1, results, back_square, back_cross, back_along, back_lift)
    return out[None, None, None]


def solution(mesh):
    placed = (P("kx", "ky", "kz", None, None, None), P("kx", "ky", "kz", None, None))
    return jax.shard_map(
        per_device,
        mesh=mesh,
        in_specs=placed,
        out_specs=P("kx", "ky", "kz", None, None, None, None),
        check_vma=False,
    )
```

```python
import jax
import jax.numpy as jnp
from jax import lax
from jax.experimental import pallas as pl
from jax.experimental.pallas import tpu as pltpu
from jax.sharding import PartitionSpec as P

AXES = ("kx", "ky", "kz")
BANDS, PARTS, WIDTH, SLABS, LANES = 128, 2, 4096, 32, 128
ROWS = BANDS * PARTS
BLOCKS = 4
PER = SLABS // BLOCKS
TAIL = 16
F32 = jnp.float32
COST = 1024
NT = (((1,), (1,)), ((), ()))
ANY = pl.BlockSpec(memory_space=pl.ANY)
VMEM = pl.BlockSpec(memory_space=pltpu.VMEM)
HBM = pl.BlockSpec(memory_space=pltpu.HBM)
RESULT = jax.ShapeDtypeStruct((PARTS, BANDS, BANDS), F32)
QUAD = jax.ShapeDtypeStruct((4, PARTS, BANDS, BANDS), F32)
RESULTS = jax.ShapeDtypeStruct((3, PARTS, BANDS, BANDS), F32)


def routes(nx, ny, nz):
    def at(a, b, c):
        return ((a % nx) * ny + b % ny) * nz + c % nz

    square, cross, along, lift = [], [], [], []
    for a in range(nx):
        for b in range(ny):
            for c in range(nz):
                me, high, core = at(a, b, c), a % 2, b % 2
                up = c - 1 if core else c + 1
                if high == core:
                    square.append((me, at(a, b - 1, c) if high else at(a, b + 1, c)))
                    cross.append((me, at(a - 1, b + 1, c) if high else at(a + 1, b - 1, c)))
                    along.append((me, at(a + 2, b, c) if high else at(a - 2, b, c)))
                    lift.append((me, at(a, b - 1 if core else b + 1, up)))
                else:
                    square.append((me, at(a - 1, b, c) if high else at(a + 1, b, c)))
                    cross.append((me, at(a, b, up)))
    return square, cross, along, lift


def back(route):
    return [(t, s) for s, t in route]


def send(x, route):
    return lax.ppermute(x, AXES, route)


def place():
    return lax.rem(lax.axis_index("kx"), 2), lax.rem(lax.axis_index("ky"), 2)


def pack_kernel(u_ref, maps_ref, out_ref, raw, ready, maps, ints, in_sems, out_sems, sem):
    width = PER * LANES
    loads = [
        pltpu.make_async_copy(u_ref.at[:, :, pl.ds(i * width, width)], raw.at[i], in_sems.at[i])
        for i in range(BLOCKS)
    ]
    stores = [
        pltpu.make_async_copy(ready.at[i], out_ref.at[pl.ds(i * PER * ROWS, PER * ROWS), :], out_sems.at[i])
        for i in range(BLOCKS)
    ]
    table = pltpu.make_async_copy(maps_ref, maps, sem)
    table.start()
    for c in loads:
        c.start()
    ints[...] = jnp.zeros_like(ints)
    table.wait()
    for d in range(maps.shape[0]):
        ints[d : d + 1, :SLABS] = maps[d]
    ready[BLOCKS, :TAIL, :] = ints[...].astype(F32).astype(jnp.bfloat16)
    tail = pltpu.make_async_copy(ready.at[BLOCKS, pl.ds(0, TAIL), :], out_ref.at[pl.ds(SLABS * ROWS, TAIL), :], sem)
    tail.start()
    for i in range(BLOCKS):
        loads[i].wait()
        for s in range(PER):
            ready[i, s * ROWS : (s + 1) * ROWS, :] = raw[i, :, :, s * LANES : (s + 1) * LANES].reshape(ROWS, LANES)
        stores[i].start()
    tail.wait()
    for c in stores:
        c.wait()


def packed(u, maps):
    return pl.pallas_call(
        pack_kernel,
        in_specs=[ANY, ANY],
        out_specs=ANY,
        out_shape=jax.ShapeDtypeStruct((SLABS * ROWS + TAIL, LANES), jnp.bfloat16),
        scratch_shapes=[
            pltpu.VMEM((BLOCKS, BANDS, PARTS, PER * LANES), jnp.bfloat16),
            pltpu.VMEM((BLOCKS + 1, PER * ROWS, LANES), jnp.bfloat16),
            pltpu.VMEM((maps.shape[0], 1, SLABS), jnp.int32),
            pltpu.VMEM((TAIL, LANES), jnp.int32),
            pltpu.SemaphoreType.DMA((BLOCKS,)),
            pltpu.SemaphoreType.DMA((BLOCKS,)),
            pltpu.SemaphoreType.DMA,
        ],
        compiler_params=pltpu.CompilerParams(vmem_limit_bytes=61 << 20),
        cost_estimate=pl.CostEstimate(flops=0, bytes_accessed=4 << 20, transcendentals=0),
    )(u, maps[:, None, :])


def keep_kernel(own, out_ref, sem):
    copy = pltpu.make_async_copy(own, out_ref, sem)
    copy.start()
    copy.wait()


def kept(own):
    return pl.pallas_call(
        keep_kernel,
        in_specs=[ANY],
        out_specs=VMEM,
        out_shape=jax.ShapeDtypeStruct(own.shape, own.dtype),
        scratch_shapes=[pltpu.SemaphoreType.DMA],
        compiler_params=pltpu.CompilerParams(vmem_limit_bytes=16 << 20),
        cost_estimate=pl.CostEstimate(flops=0, bytes_accessed=4 << 20, transcendentals=0),
    )(own)


def slab(ref, index):
    return ref[pl.ds(pl.multiple_of(index * ROWS, ROWS), ROWS), :]


def multiply(p_ref, q_ref, first, direction, ints, order, g_ref, s_ref, sem):
    tail = pl.ds(SLABS * ROWS, TAIL)
    chosen = jnp.where(first, p_ref[tail, :].astype(F32), q_ref[tail, :].astype(F32))
    rows = lax.broadcasted_iota(jnp.int32, chosen.shape, 0)
    ints[...] = jnp.sum(jnp.where(rows == direction, chosen, 0.0), axis=0, keepdims=True).astype(jnp.int32)
    copy = pltpu.make_async_copy(ints, order, sem)
    copy.start()
    copy.wait()
    left, right = [], []
    for s in range(SLABS):
        other = order[0, s]
        left.append(slab(p_ref, jnp.where(first, s, other)))
        right.append(slab(q_ref, jnp.where(first, other, s)))
    g = lax.dot_general(
        jnp.concatenate(left, axis=1), jnp.concatenate(right, axis=1), NT, preferred_element_type=F32
    )
    for half in range(2):
        g_ref[half] = g[:, half * LANES : (half + 1) * LANES]
    for half in range(2):
        for part in range(2):
            s_ref[part, half * LANES : (half + 1) * LANES] = g_ref[half, pl.ds(part, BANDS, stride=2), :].T
    rr, ri = s_ref[0, pl.ds(0, BANDS, stride=2), :], s_ref[0, pl.ds(1, BANDS, stride=2), :]
    ir, ii = s_ref[1, pl.ds(0, BANDS, stride=2), :], s_ref[1, pl.ds(1, BANDS, stride=2), :]
    return rr + ii, ri - ir


def put(t_ref, h_ref, real, imag):
    h_ref[0] = real
    h_ref[1] = -imag
    t_ref[0] = real.T
    t_ref[1] = imag.T


def square_kernel(own, square, t_ref, b_ref, *scratch):
    high, core = place()
    put(t_ref, b_ref.at[0], *multiply(own, square, core == 0, jnp.where(high == core, 0, 1), *scratch))


def cross_kernel(own, square, cross, _, b_ref, h_ref, *scratch):
    high, core = place()

    @pl.when(high == core)
    def _():
        put(b_ref.at[2], h_ref, *multiply(square, cross, high == 1, 1, *scratch))

    @pl.when(high != core)
    def _():
        put(b_ref.at[2], h_ref, *multiply(own, cross, core == 1, 2, *scratch))


def along_kernel(square, along, lift, _, b_ref, h_ref, *scratch):
    high, core = place()

    @pl.when(high == core)
    def _():
        put(b_ref.at[1], h_ref.at[0], *multiply(square, along, high == 0, 0, *scratch))

    @pl.when(high != core)
    def _():
        put(b_ref.at[1], h_ref.at[0], *multiply(square, lift, core == 0, 2, *scratch))


def multiplier(kernel, outs, buffers, results=None):
    operands = list(buffers) if results is None else [*buffers, results]
    return pl.pallas_call(
        kernel,
        in_specs=[VMEM] * len(operands),
        out_specs=[VMEM] * len(outs),
        out_shape=outs,
        input_output_aliases={} if results is None else {len(buffers): 0},
        scratch_shapes=[
            pltpu.VMEM((1, LANES), jnp.int32),
            pltpu.SMEM((1, LANES), jnp.int32),
            pltpu.VMEM((2, ROWS, LANES), F32),
            pltpu.VMEM((2, ROWS, LANES), F32),
            pltpu.SemaphoreType.DMA,
        ],
        compiler_params=pltpu.CompilerParams(vmem_limit_bytes=16 << 20),
        cost_estimate=pl.CostEstimate(
            flops=COST, bytes_accessed=COST, transcendentals=0
        ),
    )(*operands)


def gather_kernel(t1, mine, r_square, r_cross, r_lift, r_along, out_ref, sems):
    high, core = place()
    three = [r_square.at[i] for i in range(3)]
    r_along, r_lift = r_along.at[0], r_lift.at[0]
    places = {
        0: [t1, three[0], r_lift, r_along, r_cross, three[1]],
        1: [three[0], three[2], mine.at[2], three[1], t1, r_cross],
        2: [three[1], t1, r_cross, three[0], three[2], mine.at[2]],
        3: [r_along, r_cross, three[1], t1, three[0], r_lift],
    }
    for role, sources in places.items():

        @pl.when(2 * high + core == role)
        def _():
            copies = [pltpu.make_async_copy(x, out_ref.at[i], sems.at[i]) for i, x in enumerate(sources)]
            for c in copies:
                c.start()
            for c in copies:
                c.wait()


def gathered(*parts):
    return pl.pallas_call(
        gather_kernel,
        in_specs=[ANY] * len(parts),
        out_specs=ANY,
        out_shape=jax.ShapeDtypeStruct((6, PARTS, BANDS, BANDS), F32),
        scratch_shapes=[pltpu.SemaphoreType.DMA((6,))],
        compiler_params=pltpu.CompilerParams(vmem_limit_bytes=4 << 20),
        cost_estimate=pl.CostEstimate(flops=0, bytes_accessed=COST, transcendentals=0),
    )(*parts)


def per_device(coeffs, slab_maps):
    square, cross, along, lift = routes(*(lax.axis_size(a) for a in AXES))
    own = packed(coeffs[0, 0, 0], slab_maps[0, 0, 0])
    from_square = send(own, square)
    from_cross = send(own, cross)
    from_along = send(own, along)
    from_lift = send(own, lift)
    own = kept(own)
    t1, results = multiplier(square_kernel, [RESULT, RESULTS], [own, from_square])
    results, h3 = multiplier(along_kernel, [RESULTS, QUAD], [from_square, from_along, from_lift], results)
    results, h2 = multiplier(cross_kernel, [RESULTS, RESULT], [own, from_square, from_cross], results)
    back_cross = send(h2, back(cross))
    back_square = send(results, back(square))
    back_along = send(h3, back(along))
    back_lift = send(h3, back(lift))
    out = gathered(t1, results, back_square, back_cross, back_lift, back_along)
    return out[None, None, None]


def solution(mesh):
    placed = (P("kx", "ky", "kz", None, None, None), P("kx", "ky", "kz", None, None))
    return jax.shard_map(
        per_device,
        mesh=mesh,
        in_specs=placed,
        out_specs=P("kx", "ky", "kz", None, None, None, None),
        check_vma=False,
    )
```

```python
import jax
import jax.numpy as jnp
from jax import lax
from jax.experimental import pallas as pl
from jax.experimental.pallas import tpu as pltpu
from jax.sharding import PartitionSpec as P

AXES = ("kx", "ky", "kz")
BANDS, PARTS, WIDTH, SLABS, LANES = 128, 2, 4096, 32, 128
ROWS = BANDS * PARTS
BLOCKS = 4
PER = SLABS // BLOCKS
TAIL = 16
F32 = jnp.float32
COST = 1024
NT = (((1,), (1,)), ((), ()))
ANY = pl.BlockSpec(memory_space=pl.ANY)
VMEM = pl.BlockSpec(memory_space=pltpu.VMEM)
HBM = pl.BlockSpec(memory_space=pltpu.HBM)
RESULT = jax.ShapeDtypeStruct((PARTS, BANDS, BANDS), F32)
QUAD = jax.ShapeDtypeStruct((4, PARTS, BANDS, BANDS), F32)
RESULTS = jax.ShapeDtypeStruct((3, PARTS, BANDS, BANDS), F32)


def routes(nx, ny, nz):
    def at(a, b, c):
        return ((a % nx) * ny + b % ny) * nz + c % nz

    square, cross, along, lift = [], [], [], []
    for a in range(nx):
        for b in range(ny):
            for c in range(nz):
                me, high, core = at(a, b, c), a % 2, b % 2
                up = c - 1 if core else c + 1
                if high == core:
                    square.append((me, at(a, b - 1, c) if high else at(a, b + 1, c)))
                    cross.append((me, at(a - 1, b + 1, c) if high else at(a + 1, b - 1, c)))
                    along.append((me, at(a + 2, b, c) if high else at(a - 2, b, c)))
                    lift.append((me, at(a, b - 1 if core else b + 1, up)))
                else:
                    square.append((me, at(a - 1, b, c) if high else at(a + 1, b, c)))
                    cross.append((me, at(a, b, up)))
    return square, cross, along, lift


def back(route):
    return [(t, s) for s, t in route]


def send(x, route):
    return lax.ppermute(x, AXES, route)


def place():
    return lax.rem(lax.axis_index("kx"), 2), lax.rem(lax.axis_index("ky"), 2)


def pack_kernel(u_ref, maps_ref, out_ref, raw, ready, maps, ints, in_sems, out_sems, sem):
    width = PER * LANES
    loads = [
        pltpu.make_async_copy(u_ref.at[:, :, pl.ds(i * width, width)], raw.at[i], in_sems.at[i])
        for i in range(BLOCKS)
    ]
    stores = [
        pltpu.make_async_copy(ready.at[i], out_ref.at[pl.ds(i * PER * ROWS, PER * ROWS), :], out_sems.at[i])
        for i in range(BLOCKS)
    ]
    table = pltpu.make_async_copy(maps_ref, maps, sem)
    table.start()
    for c in loads:
        c.start()
    ints[...] = jnp.zeros_like(ints)
    table.wait()
    for d in range(maps.shape[0]):
        ints[d : d + 1, :SLABS] = maps[d]
    ready[BLOCKS, :TAIL, :] = ints[...].astype(F32).astype(jnp.bfloat16)
    tail = pltpu.make_async_copy(ready.at[BLOCKS, pl.ds(0, TAIL), :], out_ref.at[pl.ds(SLABS * ROWS, TAIL), :], sem)
    tail.start()
    for i in range(BLOCKS):
        loads[i].wait()
        for s in range(PER):
            ready[i, s * ROWS : (s + 1) * ROWS, :] = raw[i, :, :, s * LANES : (s + 1) * LANES].reshape(ROWS, LANES)
        stores[i].start()
    tail.wait()
    for c in stores:
        c.wait()


def packed(u, maps):
    return pl.pallas_call(
        pack_kernel,
        in_specs=[ANY, ANY],
        out_specs=ANY,
        out_shape=jax.ShapeDtypeStruct((SLABS * ROWS + TAIL, LANES), jnp.bfloat16),
        scratch_shapes=[
            pltpu.VMEM((BLOCKS, BANDS, PARTS, PER * LANES), jnp.bfloat16),
            pltpu.VMEM((BLOCKS + 1, PER * ROWS, LANES), jnp.bfloat16),
            pltpu.VMEM((maps.shape[0], 1, SLABS), jnp.int32),
            pltpu.VMEM((TAIL, LANES), jnp.int32),
            pltpu.SemaphoreType.DMA((BLOCKS,)),
            pltpu.SemaphoreType.DMA((BLOCKS,)),
            pltpu.SemaphoreType.DMA,
        ],
        compiler_params=pltpu.CompilerParams(vmem_limit_bytes=61 << 20),
        cost_estimate=pl.CostEstimate(flops=0, bytes_accessed=4 << 20, transcendentals=0),
    )(u, maps[:, None, :])


def keep_kernel(own, out_ref, sem):
    copy = pltpu.make_async_copy(own, out_ref, sem)
    copy.start()
    copy.wait()


def kept(own):
    return pl.pallas_call(
        keep_kernel,
        in_specs=[ANY],
        out_specs=VMEM,
        out_shape=jax.ShapeDtypeStruct(own.shape, own.dtype),
        scratch_shapes=[pltpu.SemaphoreType.DMA],
        compiler_params=pltpu.CompilerParams(vmem_limit_bytes=16 << 20),
        cost_estimate=pl.CostEstimate(flops=0, bytes_accessed=4 << 20, transcendentals=0),
    )(own)


def token_kernel(_, out_ref):
    out_ref[...] = jnp.zeros_like(out_ref)


def token(array):
    return pl.pallas_call(
        token_kernel,
        in_specs=[ANY],
        out_specs=VMEM,
        out_shape=jax.ShapeDtypeStruct((8, LANES), F32),
        cost_estimate=pl.CostEstimate(flops=COST, bytes_accessed=COST, transcendentals=0),
    )(array)


def slab(ref, index):
    return ref[pl.ds(pl.multiple_of(index * ROWS, ROWS), ROWS), :]


def multiply(p_ref, q_ref, first, direction, ints, order, g_ref, s_ref, sem):
    tail = pl.ds(SLABS * ROWS, TAIL)
    chosen = jnp.where(first, p_ref[tail, :].astype(F32), q_ref[tail, :].astype(F32))
    rows = lax.broadcasted_iota(jnp.int32, chosen.shape, 0)
    ints[...] = jnp.sum(jnp.where(rows == direction, chosen, 0.0), axis=0, keepdims=True).astype(jnp.int32)
    copy = pltpu.make_async_copy(ints, order, sem)
    copy.start()
    copy.wait()
    left, right = [], []
    for s in range(SLABS):
        other = order[0, s]
        left.append(slab(p_ref, jnp.where(first, s, other)))
        right.append(slab(q_ref, jnp.where(first, other, s)))
    g = lax.dot_general(
        jnp.concatenate(left, axis=1), jnp.concatenate(right, axis=1), NT, preferred_element_type=F32
    )
    for half in range(2):
        g_ref[half] = g[:, half * LANES : (half + 1) * LANES]
    for half in range(2):
        for part in range(2):
            s_ref[part, half * LANES : (half + 1) * LANES] = g_ref[half, pl.ds(part, BANDS, stride=2), :].T
    rr, ri = s_ref[0, pl.ds(0, BANDS, stride=2), :], s_ref[0, pl.ds(1, BANDS, stride=2), :]
    ir, ii = s_ref[1, pl.ds(0, BANDS, stride=2), :], s_ref[1, pl.ds(1, BANDS, stride=2), :]
    return rr + ii, ri - ir


def put(t_ref, h_ref, real, imag):
    h_ref[0] = real
    h_ref[1] = -imag
    t_ref[0] = real.T
    t_ref[1] = imag.T


def square_kernel(_, own, square, t_ref, b_ref, *scratch):
    high, core = place()
    put(t_ref, b_ref.at[0], *multiply(own, square, core == 0, jnp.where(high == core, 0, 1), *scratch))


def cross_kernel(own, square, cross, _, b_ref, h_ref, *scratch):
    high, core = place()

    @pl.when(high == core)
    def _():
        put(b_ref.at[2], h_ref, *multiply(square, cross, high == 1, 1, *scratch))

    @pl.when(high != core)
    def _():
        put(b_ref.at[2], h_ref, *multiply(own, cross, core == 1, 2, *scratch))


def along_kernel(square, along, lift, _, b_ref, h_ref, *scratch):
    high, core = place()

    @pl.when(high == core)
    def _():
        put(b_ref.at[1], h_ref.at[0], *multiply(square, along, high == 0, 0, *scratch))

    @pl.when(high != core)
    def _():
        put(b_ref.at[1], h_ref.at[0], *multiply(square, lift, core == 0, 2, *scratch))


def multiplier(kernel, outs, buffers, results=None):
    operands = list(buffers) if results is None else [*buffers, results]
    return pl.pallas_call(
        kernel,
        in_specs=[VMEM] * len(operands),
        out_specs=[VMEM] * len(outs),
        out_shape=outs,
        input_output_aliases={} if results is None else {len(buffers): 0},
        scratch_shapes=[
            pltpu.VMEM((1, LANES), jnp.int32),
            pltpu.SMEM((1, LANES), jnp.int32),
            pltpu.VMEM((2, ROWS, LANES), F32),
            pltpu.VMEM((2, ROWS, LANES), F32),
            pltpu.SemaphoreType.DMA,
        ],
        compiler_params=pltpu.CompilerParams(vmem_limit_bytes=16 << 20),
        cost_estimate=pl.CostEstimate(
            flops=COST, bytes_accessed=COST, transcendentals=0
        ),
    )(*operands)


def gather_kernel(t1, mine, r_square, r_cross, r_lift, r_along, out_ref, sems):
    high, core = place()
    three = [r_square.at[i] for i in range(3)]
    r_along, r_lift = r_along.at[0], r_lift.at[0]
    places = {
        0: [t1, three[0], r_lift, r_along, r_cross, three[1]],
        1: [three[0], three[2], mine.at[2], three[1], t1, r_cross],
        2: [three[1], t1, r_cross, three[0], three[2], mine.at[2]],
        3: [r_along, r_cross, three[1], t1, three[0], r_lift],
    }
    for role, sources in places.items():

        @pl.when(2 * high + core == role)
        def _():
            copies = [pltpu.make_async_copy(x, out_ref.at[i], sems.at[i]) for i, x in enumerate(sources)]
            for c in copies:
                c.start()
            for c in copies:
                c.wait()


def gathered(*parts):
    return pl.pallas_call(
        gather_kernel,
        in_specs=[ANY] * len(parts),
        out_specs=ANY,
        out_shape=jax.ShapeDtypeStruct((6, PARTS, BANDS, BANDS), F32),
        scratch_shapes=[pltpu.SemaphoreType.DMA((6,))],
        compiler_params=pltpu.CompilerParams(vmem_limit_bytes=4 << 20),
        cost_estimate=pl.CostEstimate(flops=0, bytes_accessed=COST, transcendentals=0),
    )(*parts)


def per_device(coeffs, slab_maps):
    square, cross, along, lift = routes(*(lax.axis_size(a) for a in AXES))
    own = packed(coeffs[0, 0, 0], slab_maps[0, 0, 0])
    from_lift = send(own, lift)
    from_square = send(own, square)
    from_cross = send(own, cross)
    from_along = send(own, along)
    own = kept(own)
    t1, results = multiplier(square_kernel, [RESULT, RESULTS], [token(from_lift), own, from_square])
    results, h3 = multiplier(along_kernel, [RESULTS, QUAD], [from_square, from_along, from_lift], results)
    results, h2 = multiplier(cross_kernel, [RESULTS, RESULT], [own, from_square, from_cross], results)
    back_cross = send(h2, back(cross))
    back_square = send(results, back(square))
    back_along = send(h3, back(along))
    back_lift = send(h3, back(lift))
    out = gathered(t1, results, back_square, back_cross, back_lift, back_along)
    return out[None, None, None]


def solution(mesh):
    placed = (P("kx", "ky", "kz", None, None, None), P("kx", "ky", "kz", None, None))
    return jax.shard_map(
        per_device,
        mesh=mesh,
        in_specs=placed,
        out_specs=P("kx", "ky", "kz", None, None, None, None),
        check_vma=False,
    )
```

```python
import jax
import jax.numpy as jnp
from jax import lax
from jax.experimental import pallas as pl
from jax.experimental.pallas import tpu as pltpu
from jax.sharding import PartitionSpec as P

AXES = ("kx", "ky", "kz")
BANDS, PARTS, WIDTH, SLABS, LANES = 128, 2, 4096, 32, 128
ROWS = BANDS * PARTS
BLOCKS = 2
PER = SLABS // BLOCKS
TAIL = 16
F32 = jnp.float32
COST = 1024
NT = (((1,), (1,)), ((), ()))
ANY = pl.BlockSpec(memory_space=pl.ANY)
VMEM = pl.BlockSpec(memory_space=pltpu.VMEM)
HBM = pl.BlockSpec(memory_space=pltpu.HBM)
RESULT = jax.ShapeDtypeStruct((PARTS, BANDS, BANDS), F32)
QUAD = jax.ShapeDtypeStruct((4, PARTS, BANDS, BANDS), F32)
RESULTS = jax.ShapeDtypeStruct((3, PARTS, BANDS, BANDS), F32)


def routes(nx, ny, nz):
    def at(a, b, c):
        return ((a % nx) * ny + b % ny) * nz + c % nz

    square, cross, along, lift = [], [], [], []
    for a in range(nx):
        for b in range(ny):
            for c in range(nz):
                me, high, core = at(a, b, c), a % 2, b % 2
                up = c - 1 if core else c + 1
                if high == core:
                    square.append((me, at(a, b - 1, c) if high else at(a, b + 1, c)))
                    cross.append((me, at(a - 1, b + 1, c) if high else at(a + 1, b - 1, c)))
                    along.append((me, at(a + 2, b, c) if high else at(a - 2, b, c)))
                    lift.append((me, at(a, b - 1 if core else b + 1, up)))
                else:
                    square.append((me, at(a - 1, b, c) if high else at(a + 1, b, c)))
                    cross.append((me, at(a, b, up)))
    return square, cross, along, lift


def back(route):
    return [(t, s) for s, t in route]


def send(x, route):
    return lax.ppermute(x, AXES, route)


def place():
    return lax.rem(lax.axis_index("kx"), 2), lax.rem(lax.axis_index("ky"), 2)


def pack_kernel(u_ref, maps_ref, out_ref, raw, ready, maps, ints, in_sems, out_sems, sem):
    width = PER * LANES
    loads = [
        pltpu.make_async_copy(u_ref.at[:, :, pl.ds(i * width, width)], raw.at[i], in_sems.at[i])
        for i in range(BLOCKS)
    ]
    stores = [
        pltpu.make_async_copy(ready.at[i], out_ref.at[pl.ds(i * PER * ROWS, PER * ROWS), :], out_sems.at[i])
        for i in range(BLOCKS)
    ]
    table = pltpu.make_async_copy(maps_ref, maps, sem)
    table.start()
    for c in loads:
        c.start()
    ints[...] = jnp.zeros_like(ints)
    table.wait()
    for d in range(maps.shape[0]):
        ints[d : d + 1, :SLABS] = maps[d]
    ready[BLOCKS, :TAIL, :] = ints[...].astype(F32).astype(jnp.bfloat16)
    tail = pltpu.make_async_copy(ready.at[BLOCKS, pl.ds(0, TAIL), :], out_ref.at[pl.ds(SLABS * ROWS, TAIL), :], sem)
    tail.start()
    for i in range(BLOCKS):
        loads[i].wait()
        for s in range(PER):
            ready[i, s * ROWS : (s + 1) * ROWS, :] = raw[i, :, :, s * LANES : (s + 1) * LANES].reshape(ROWS, LANES)
        stores[i].start()
    tail.wait()
    for c in stores:
        c.wait()


def packed(u, maps):
    return pl.pallas_call(
        pack_kernel,
        in_specs=[ANY, ANY],
        out_specs=ANY,
        out_shape=jax.ShapeDtypeStruct((SLABS * ROWS + TAIL, LANES), jnp.bfloat16),
        scratch_shapes=[
            pltpu.VMEM((BLOCKS, BANDS, PARTS, PER * LANES), jnp.bfloat16),
            pltpu.VMEM((BLOCKS + 1, PER * ROWS, LANES), jnp.bfloat16),
            pltpu.VMEM((maps.shape[0], 1, SLABS), jnp.int32),
            pltpu.VMEM((TAIL, LANES), jnp.int32),
            pltpu.SemaphoreType.DMA((BLOCKS,)),
            pltpu.SemaphoreType.DMA((BLOCKS,)),
            pltpu.SemaphoreType.DMA,
        ],
        compiler_params=pltpu.CompilerParams(vmem_limit_bytes=61 << 20),
        cost_estimate=pl.CostEstimate(flops=0, bytes_accessed=4 << 20, transcendentals=0),
    )(u, maps[:, None, :])


def keep_kernel(own, out_ref, sem):
    copy = pltpu.make_async_copy(own, out_ref, sem)
    copy.start()
    copy.wait()


def kept(own):
    return pl.pallas_call(
        keep_kernel,
        in_specs=[ANY],
        out_specs=VMEM,
        out_shape=jax.ShapeDtypeStruct(own.shape, own.dtype),
        scratch_shapes=[pltpu.SemaphoreType.DMA],
        compiler_params=pltpu.CompilerParams(vmem_limit_bytes=16 << 20),
        cost_estimate=pl.CostEstimate(flops=0, bytes_accessed=4 << 20, transcendentals=0),
    )(own)


def slab(ref, index):
    return ref[pl.ds(pl.multiple_of(index * ROWS, ROWS), ROWS), :]


def multiply(p_ref, q_ref, first, direction, ints, order, g_ref, s_ref, sem):
    tail = pl.ds(SLABS * ROWS, TAIL)
    chosen = jnp.where(first, p_ref[tail, :].astype(F32), q_ref[tail, :].astype(F32))
    rows = lax.broadcasted_iota(jnp.int32, chosen.shape, 0)
    ints[...] = jnp.sum(jnp.where(rows == direction, chosen, 0.0), axis=0, keepdims=True).astype(jnp.int32)
    copy = pltpu.make_async_copy(ints, order, sem)
    copy.start()
    copy.wait()
    left, right = [], []
    for s in range(SLABS):
        other = order[0, s]
        left.append(slab(p_ref, jnp.where(first, s, other)))
        right.append(slab(q_ref, jnp.where(first, other, s)))
    g = lax.dot_general(
        jnp.concatenate(left, axis=1), jnp.concatenate(right, axis=1), NT, preferred_element_type=F32
    )
    for half in range(2):
        g_ref[half] = g[:, half * LANES : (half + 1) * LANES]
    for half in range(2):
        for part in range(2):
            s_ref[part, half * LANES : (half + 1) * LANES] = g_ref[half, pl.ds(part, BANDS, stride=2), :].T
    rr, ri = s_ref[0, pl.ds(0, BANDS, stride=2), :], s_ref[0, pl.ds(1, BANDS, stride=2), :]
    ir, ii = s_ref[1, pl.ds(0, BANDS, stride=2), :], s_ref[1, pl.ds(1, BANDS, stride=2), :]
    return rr + ii, ri - ir


def put(t_ref, h_ref, real, imag):
    h_ref[0] = real
    h_ref[1] = -imag
    t_ref[0] = real.T
    t_ref[1] = imag.T


def square_kernel(own, square, t_ref, b_ref, *scratch):
    high, core = place()
    put(t_ref, b_ref.at[0], *multiply(own, square, core == 0, jnp.where(high == core, 0, 1), *scratch))


def cross_kernel(own, square, cross, _, b_ref, h_ref, *scratch):
    high, core = place()

    @pl.when(high == core)
    def _():
        put(b_ref.at[2], h_ref, *multiply(square, cross, high == 1, 1, *scratch))

    @pl.when(high != core)
    def _():
        put(b_ref.at[2], h_ref, *multiply(own, cross, core == 1, 2, *scratch))


def along_kernel(square, along, lift, _, b_ref, h_ref, *scratch):
    high, core = place()

    @pl.when(high == core)
    def _():
        put(b_ref.at[1], h_ref.at[0], *multiply(square, along, high == 0, 0, *scratch))

    @pl.when(high != core)
    def _():
        put(b_ref.at[1], h_ref.at[0], *multiply(square, lift, core == 0, 2, *scratch))


def multiplier(kernel, outs, buffers, results=None):
    operands = list(buffers) if results is None else [*buffers, results]
    return pl.pallas_call(
        kernel,
        in_specs=[VMEM] * len(operands),
        out_specs=[VMEM] * len(outs),
        out_shape=outs,
        input_output_aliases={} if results is None else {len(buffers): 0},
        scratch_shapes=[
            pltpu.VMEM((1, LANES), jnp.int32),
            pltpu.SMEM((1, LANES), jnp.int32),
            pltpu.VMEM((2, ROWS, LANES), F32),
            pltpu.VMEM((2, ROWS, LANES), F32),
            pltpu.SemaphoreType.DMA,
        ],
        compiler_params=pltpu.CompilerParams(vmem_limit_bytes=16 << 20),
        cost_estimate=pl.CostEstimate(
            flops=COST, bytes_accessed=COST, transcendentals=0
        ),
    )(*operands)


def gather_kernel(t1, mine, r_square, r_cross, r_lift, r_along, out_ref, sems):
    high, core = place()
    three = [r_square.at[i] for i in range(3)]
    r_along, r_lift = r_along.at[0], r_lift.at[0]
    places = {
        0: [t1, three[0], r_lift, r_along, r_cross, three[1]],
        1: [three[0], three[2], mine.at[2], three[1], t1, r_cross],
        2: [three[1], t1, r_cross, three[0], three[2], mine.at[2]],
        3: [r_along, r_cross, three[1], t1, three[0], r_lift],
    }
    for role, sources in places.items():

        @pl.when(2 * high + core == role)
        def _():
            copies = [pltpu.make_async_copy(x, out_ref.at[i], sems.at[i]) for i, x in enumerate(sources)]
            for c in copies:
                c.start()
            for c in copies:
                c.wait()


def gathered(*parts):
    return pl.pallas_call(
        gather_kernel,
        in_specs=[ANY] * len(parts),
        out_specs=ANY,
        out_shape=jax.ShapeDtypeStruct((6, PARTS, BANDS, BANDS), F32),
        scratch_shapes=[pltpu.SemaphoreType.DMA((6,))],
        compiler_params=pltpu.CompilerParams(vmem_limit_bytes=4 << 20),
        cost_estimate=pl.CostEstimate(flops=0, bytes_accessed=COST, transcendentals=0),
    )(*parts)


def per_device(coeffs, slab_maps):
    square, cross, along, lift = routes(*(lax.axis_size(a) for a in AXES))
    own = packed(coeffs[0, 0, 0], slab_maps[0, 0, 0])
    from_square = send(own, square)
    from_cross = send(own, cross)
    from_along = send(own, along)
    from_lift = send(own, lift)
    own = kept(own)
    t1, results = multiplier(square_kernel, [RESULT, RESULTS], [own, from_square])
    results, h3 = multiplier(along_kernel, [RESULTS, QUAD], [from_square, from_along, from_lift], results)
    results, h2 = multiplier(cross_kernel, [RESULTS, RESULT], [own, from_square, from_cross], results)
    back_cross = send(h2, back(cross))
    back_square = send(results, back(square))
    back_along = send(h3, back(along))
    back_lift = send(h3, back(lift))
    out = gathered(t1, results, back_square, back_cross, back_lift, back_along)
    return out[None, None, None]


def solution(mesh):
    placed = (P("kx", "ky", "kz", None, None, None), P("kx", "ky", "kz", None, None))
    return jax.shard_map(
        per_device,
        mesh=mesh,
        in_specs=placed,
        out_specs=P("kx", "ky", "kz", None, None, None, None),
        check_vma=False,
    )
```
